128 devices in a mesh: space: 8 (over x, core), tm: 16 (over z, y).
Axes of the slice: x: 4, y: 4, z: 4, core: 2. Of those that a mesh axis runs over, the one named last changes fastest.
Arguments:
- snapshots: bfloat16 [8192, 131072], P('tm', 'space'), may hold values from -24 to 24
- freq_bins: int32 [2], replicated, may hold values from 1 to 127
Outputs:
- gram_matrix: float32 [2, 128, 128], replicated
- whitened: float32 [2, 128, 131072], P(None, None, ('space', 'tm'))
The draws below stay inside these ranges and needn't reach their ends.
All inputs are finite; a program needn't handle non-finite values.
Results may differ from the reference program's by a relative error of at most 0.0041.
Values may be sent and summed in bfloat16 or wider, within the bound.
A program may use at most 128 MiB of HBM per device.

```python
import math
import jax
import jax.numpy as jnp
from jax import lax

NFFT = 256
HOP = 128
NF = 2
NT = 8192
NGRID = 131072
NB = 64


def draw_snapshots(key, part):
    keys = jax.random.split(jax.random.fold_in(key, 17), 2)
    position = jnp.arange(NGRID, dtype=jnp.float32) / NGRID
    rough = jnp.exp(jax.random.uniform(keys[1], (NGRID,), jnp.float32, 0.0, math.log(10.0)))
    amplitude = jnp.power(3.0, position) * rough / 8.0
    noise = jnp.clip(jax.random.normal(keys[0], (NT, NGRID), jnp.float32), -5.0, 5.0)
    values = noise * amplitude[None, :]
    return jnp.clip(values, -24.0, 24.0).astype(jnp.bfloat16)


def setup_inputs(seed: int = 0) -> dict:
    arg_keys = jax.random.split(jax.random.key(seed), 3)
    snapshots = draw_snapshots(jax.random.fold_in(arg_keys[2], 71), 0)
    freq_bins = jax.random.randint(arg_keys[1], (NF,), 1, HOP).astype(jnp.int32)
    return dict(snapshots=snapshots, freq_bins=freq_bins)


ridge_term = 0.01

def make_table(freq_bins):
    sample = jnp.arange(NFFT, dtype=jnp.int32)
    sample_f = sample.astype(jnp.float32)
    hann_taper = 0.5 - 0.5 * jnp.cos(2.0 * jnp.pi * sample_f / NFFT)
    window = hann_taper / jnp.sqrt(jnp.sum(hann_taper * hann_taper))
    phase_idx = freq_bins[:, None] * sample[None, :] % NFFT
    angles = 2.0 * jnp.pi * phase_idx.astype(jnp.float32) / NFFT
    table = jnp.stack([window * jnp.cos(angles), -window * jnp.sin(angles)], axis=1)
    return table.astype(jnp.bfloat16)

def reference(snapshots, freq_bins):
    table_rows = make_table(freq_bins).astype(jnp.float32).reshape(NF * 2, NFFT)
    halves = snapshots.reshape(NB, HOP, NGRID)

    def one_block(block_idx):
        first = lax.dynamic_index_in_dim(halves, block_idx, 0, keepdims=False).astype(jnp.float32)
        second = lax.dynamic_index_in_dim(halves, (block_idx + 1) % NB, 0, keepdims=False).astype(jnp.float32)
        lead_part = jnp.dot(table_rows[:, :HOP].astype(jnp.float32), first.astype(jnp.float32), precision=lax.Precision.HIGHEST, preferred_element_type=jnp.float32)
        trail_part = jnp.dot(table_rows[:, HOP:].astype(jnp.float32), second.astype(jnp.float32), precision=lax.Precision.HIGHEST, preferred_element_type=jnp.float32)
        return lead_part + trail_part
    stacked = lax.map(one_block, jnp.arange(NB, dtype=jnp.int32))
    coeffs = jnp.transpose(stacked, (1, 0, 2)).reshape(NF, 2 * NB, NGRID)
    gram_matrix = jnp.einsum('fcp,fdp->fcd', coeffs, coeffs, precision=lax.Precision.HIGHEST) / NGRID
    identity = jnp.eye(2 * NB, dtype=gram_matrix.dtype)
    factor = jnp.linalg.cholesky(gram_matrix + ridge_term * identity[None])
    whitened = lax.linalg.triangular_solve(factor, coeffs, left_side=True, lower=True)
    return (gram_matrix, whitened)
```

```python
import functools
import math

import jax
import jax.numpy as jnp
from jax import lax
from jax.experimental import pallas as pl
from jax.experimental.pallas import tpu as pltpu
from jax.sharding import PartitionSpec as P

NFFT = 256
HOP = 128
NF = 2
NB = 64
COLS = 2 * NB
ROWS = NF * COLS
TM = 16
SPACE = 8
OWN = NB // TM
WIDTH = 1024
GROUPS = 4
PACK = WIDTH // GROUPS
MESH = pl.DeviceIdType.MESH
VMEM = pltpu.VMEM
ridge_term = 0.01

STEPS = (
    (2, 2), (1, 2), (2, 1), (3, 2), (2, 3), (1, 1), (3, 3), (1, 3),
    (3, 1), (0, 2), (2, 0), (0, 1), (1, 0), (0, 3), (3, 0), (0, 0),
)


def iota(shape, dim):
    return lax.broadcasted_iota(jnp.int32, shape, dim)


def base_table(freq_ref, f_of_row, r_of_row):
    shape = (16, NFFT)
    t = iota(shape, 1)
    bins = jnp.where(f_of_row == 0, freq_ref[0], freq_ref[1])
    phase = (bins * t + 64 * r_of_row) & (NFFT - 1)
    wave = jnp.cos(2.0 * math.pi * phase.astype(jnp.float32) / NFFT)
    hann = 0.5 - 0.5 * jnp.cos(2.0 * math.pi * t.astype(jnp.float32) / NFFT)
    return hann * (1.0 / math.sqrt(0.375 * NFFT)) * wave


def banded_table(freq_ref):
    row = iota((16, NFFT), 0)
    main = base_table(freq_ref, row // 8, (row // 4) % 2)
    halo = base_table(freq_ref, (row // 2) % 2, row % 2)
    j = iota((16, HOP), 0) % 4
    zero = jnp.zeros((16, HOP), jnp.float32)
    top = [
        jnp.where(j == q, main[:, :HOP], jnp.where(j == q - 1, main[:, HOP:], zero)) for q in range(OWN)
    ]
    bottom = [halo[:, HOP:], zero, zero, zero]
    return jnp.concatenate(
        [jnp.concatenate(top, axis=1), jnp.concatenate(bottom, axis=1)], axis=0
    ).astype(jnp.bfloat16)


def spread_matrices():
    out = iota((ROWS, 256), 0)
    src = iota((ROWS, 256), 1)
    f, r, s, j = out // 128, (out // 64) % 2, (out // 4) % 16, out % 4
    main = src == s * 16 + f * 8 + r * 4 + j
    tails = []
    for g in range(GROUPS):
        tails.append((j == 3) & (src == ((s + 1) % 16) * 16 + g * 4 + f * 2 + r))
    one = lambda m: jnp.where(m, 1.0, 0.0).astype(jnp.bfloat16)
    return one(main), [one(m) for m in tails]


def dot(a, b, contract=((1,), (0,))):
    return lax.dot_general(a, b, (contract, ((), ())), preferred_element_type=jnp.float32)


def gather_kernel(
    snap_ref, freq_ref, cols_ref, gram_ref,
    x_buf, send_buf, recv_buf, gpart, grecv, srecv,
    x_sem, send_sem, recv_sem, g_send, g_recv, s_send, s_recv, a_send, a_recv,
):
    sp = lax.axis_index("space")
    me = lax.axis_index("tm")
    z, y = me // 4, me % 4
    peers = [((z + dz) % 4) * 4 + (y + dy) % 4 for dz, dy in STEPS]
    mates = [(sp + k) % SPACE for k in range(1, SPACE)]

    loads = []
    for k, dest in enumerate(peers):
        cols = pl.ds(pl.multiple_of(dest * WIDTH, WIDTH), WIDTH)
        loads.append(pltpu.make_async_copy(snap_ref.at[:, cols], x_buf.at[k], x_sem.at[k]))
        loads[-1].start()

    barrier = pltpu.get_barrier_semaphore()
    for dest in peers[:-1]:
        pl.semaphore_signal(barrier, inc=1, device_id=(sp, dest), device_id_type=MESH)
    for mate in mates:
        pl.semaphore_signal(barrier, inc=1, device_id=(mate, me), device_id_type=MESH)

    table = banded_table(freq_ref)
    group = iota((16, PACK), 0) // 4
    sends = []
    for k, dest in enumerate(peers):
        loads[k].wait()
        rows = dot(table, x_buf[k])
        tail = rows[16:, :PACK]
        for g in range(1, GROUPS):
            tail = jnp.where(group == g, rows[16:, g * PACK : (g + 1) * PACK], tail)
        block = jnp.concatenate([rows[:16], tail], axis=1).astype(jnp.bfloat16)
        if k == TM - 1:
            recv_buf[me] = block
            break
        send_buf[k] = block
        if k == 0:
            pl.semaphore_wait(barrier, TM - 1 + SPACE - 1)
        copy = pltpu.make_async_remote_copy(
            src_ref=send_buf.at[k],
            dst_ref=recv_buf.at[me],
            send_sem=send_sem.at[k],
            recv_sem=recv_sem.at[k],
            device_id=(sp, dest),
            device_id_type=MESH,
        )
        copy.start()
        sends.append(copy)

    main, tails = spread_matrices()
    for copy in sends:
        copy.wait_recv()

    for g in range(GROUPS):
        lanes = slice(g * PACK, (g + 1) * PACK)
        got = recv_buf[:, :, lanes].reshape(ROWS, PACK)
        extra = recv_buf[:, :, WIDTH:].reshape(ROWS, PACK)
        cols_ref[:, lanes] = dot(main, got) + dot(tails[g], extra)
    for f in range(NF):
        values = cols_ref[f * COLS : (f + 1) * COLS, :]
        high = values.astype(jnp.bfloat16)
        low = (values - high.astype(jnp.float32)).astype(jnp.bfloat16)
        cross = dot(high, low, ((1,), (1,)))
        part = (dot(high, high, ((1,), (1,))) + (cross + cross.T)) * (1.0 / (WIDTH * TM * SPACE))
        gpart[f * 8 : (f + 1) * 8] = part.reshape(8, 16, COLS)

    copies = []
    for k, dest in enumerate(peers[:-1]):
        copy = pltpu.make_async_remote_copy(
            src_ref=gpart.at[dest],
            dst_ref=grecv.at[me],
            send_sem=g_send.at[k],
            recv_sem=g_recv.at[k],
            device_id=(sp, dest),
            device_id_type=MESH,
        )
        copy.start()
        copies.append(copy)
    grecv[me] = gpart[me]
    for copy in copies:
        copy.wait_recv()
    sends += copies
    srecv[sp] = jnp.sum(grecv[...], axis=0)

    copies = []
    for k, mate in enumerate(mates):
        copy = pltpu.make_async_remote_copy(
            src_ref=srecv.at[sp],
            dst_ref=srecv.at[sp],
            send_sem=s_send.at[k],
            recv_sem=s_recv.at[k],
            device_id=(mate, me),
            device_id_type=MESH,
        )
        copy.start()
        copies.append(copy)
    for copy in copies:
        copy.wait_recv()
    sends += copies
    gram_ref[me] = jnp.sum(srecv[...], axis=0)

    copies = []
    for k, dest in enumerate(peers[:-1]):
        copy = pltpu.make_async_remote_copy(
            src_ref=gram_ref.at[me],
            dst_ref=gram_ref.at[me],
            send_sem=a_send.at[k],
            recv_sem=a_recv.at[k],
            device_id=(sp, dest),
            device_id_type=MESH,
        )
        copy.start()
        copies.append(copy)
    for copy in copies:
        copy.wait_recv()
    sends += copies
    for copy in sends:
        copy.wait_send()


def split3(x):
    high = x.astype(jnp.bfloat16).astype(jnp.float32)
    rest = x - high
    mid = rest.astype(jnp.bfloat16).astype(jnp.float32)
    return high, mid, rest - mid


def eliminate(work_ref, inv_ref, f, b):
    base = 8 * b
    wide = 2 * COLS
    rows = [jnp.broadcast_to(work_ref[f, base + i : base + i + 1, :], (8, wide)) for i in range(8)]
    e = [
        [jnp.broadcast_to(rows[i][:, base + k : base + k + 1], (8, COLS)) for k in range(i + 1)]
        for i in range(8)
    ]
    for k in range(8):
        inv = lax.rsqrt(e[k][k])
        inv2 = jnp.concatenate([inv, inv], axis=1)
        rows[k] = rows[k] * inv2
        col = {i: e[i][k] * inv for i in range(k + 1, 8)}
        for i in range(k + 1, 8):
            for m in range(k + 1, i + 1):
                e[i][m] = e[i][m] - col[i] * col[m]
            rows[i] = rows[i] - jnp.concatenate([col[i], col[i]], axis=1) * rows[k]
    sub = iota((8, wide), 0)
    done = rows[0]
    for i in range(1, 8):
        done = jnp.where(sub == i, rows[i], done)
    inv_ref[f, base : base + 8, :] = done[:, COLS:]
    if base + 8 == COLS:
        return
    h, m, l = split3(done)
    left = jnp.concatenate([h, h, m, m, h, l], axis=0)[:, :COLS].astype(jnp.bfloat16)
    right = jnp.concatenate([h, m, h, m, l, h], axis=0).astype(jnp.bfloat16)
    update = dot(left, right, ((0,), (0,)))
    work_ref[f, base + 8 :, :] = work_ref[f, base + 8 :, :] - update[base + 8 :, :]


def whiten_kernel(gram_in, cols_ref, gram_ref, out_ref, work_ref, inv_ref):
    gram_ref[...] = gram_in[...]
    eye = jnp.where(iota((COLS, COLS), 0) == iota((COLS, COLS), 1), 1.0, 0.0)
    for f in range(NF):
        work_ref[f, :, :COLS] = gram_in[f] + ridge_term * eye
        work_ref[f, :, COLS:] = eye
    for b in range(COLS // 8):
        for f in range(NF):
            eliminate(work_ref, inv_ref, f, b)
    for f in range(NF):
        w = inv_ref[f]
        w_high = w.astype(jnp.bfloat16)
        w_low = (w - w_high.astype(jnp.float32)).astype(jnp.bfloat16)
        values = cols_ref[f * COLS : (f + 1) * COLS, :]
        high = values.astype(jnp.bfloat16)
        low = (values - high.astype(jnp.float32)).astype(jnp.bfloat16)
        out_ref[f] = dot(w_high, high) + (dot(w_low, high) + dot(w_high, low))


def on_device(snapshots, freq_bins):
    points = snapshots.shape[1]
    dma = pltpu.SemaphoreType.DMA
    vmem = pl.BlockSpec(memory_space=VMEM)
    cols, gram = pl.pallas_call(
        gather_kernel,
        out_shape=[
            jax.ShapeDtypeStruct((ROWS, WIDTH), jnp.float32),
            jax.ShapeDtypeStruct((TM, 16, COLS), jnp.float32),
        ],
        in_specs=[pl.BlockSpec(memory_space=pl.ANY), pl.BlockSpec(memory_space=pltpu.SMEM)],
        out_specs=[vmem, vmem],
        scratch_shapes=[
            VMEM((TM, TM * 32, WIDTH), jnp.bfloat16),
            VMEM((TM, 16, WIDTH + PACK), jnp.bfloat16),
            VMEM((TM, 16, WIDTH + PACK), jnp.bfloat16),
            VMEM((TM, 16, COLS), jnp.float32),
            VMEM((TM, 16, COLS), jnp.float32),
            VMEM((SPACE, 16, COLS), jnp.float32),
            dma((TM,)),
            dma((TM - 1,)),
            dma((TM - 1,)),
            dma((TM - 1,)),
            dma((TM - 1,)),
            dma((SPACE - 1,)),
            dma((SPACE - 1,)),
            dma((TM - 1,)),
            dma((TM - 1,)),
        ],
        compiler_params=pltpu.CompilerParams(
            collective_id=0, has_side_effects=True, vmem_limit_bytes=48 * 2**20
        ),
        name="gather",
    )(snapshots, freq_bins)
    gram_matrix, whitened = pl.pallas_call(
        whiten_kernel,
        out_shape=[
            jax.ShapeDtypeStruct((NF, COLS, COLS), jnp.float32),
            jax.ShapeDtypeStruct((NF, COLS, WIDTH), jnp.float32),
        ],
        in_specs=[vmem, vmem],
        out_specs=[vmem, vmem],
        scratch_shapes=[
            VMEM((NF, COLS, 2 * COLS), jnp.float32),
            VMEM((NF, COLS, COLS), jnp.float32),
        ],
        compiler_params=pltpu.CompilerParams(vmem_limit_bytes=32 * 2**20),
        name="whiten",
    )(gram.reshape(NF, COLS, COLS), cols)
    return gram_matrix, whitened


def solution(mesh):
    placed = (P("tm", "space"), P())
    return jax.shard_map(
        on_device,
        mesh=mesh,
        in_specs=placed,
        out_specs=(P(), P(None, None, ("space", "tm"))),
        check_vma=False,
    )
```

```python
import math

import jax
import jax.numpy as jnp
from jax import lax
from jax.experimental import pallas as pl
from jax.experimental.pallas import tpu as pltpu
from jax.sharding import PartitionSpec as P

NFFT = 256
HOP = 128
NF = 2
NB = 64
COLS = 2 * NB
ROWS = NF * COLS
TM = 16
SPACE = 8
OWN = NB // TM
WIDTH = 1024
GROUPS = 4
PACK = WIDTH // GROUPS
MESH = pl.DeviceIdType.MESH
VMEM = pltpu.VMEM
ridge_term = 0.01
ENTER_AT = 8
PANEL = 16

STEPS = (
    (2, 2), (1, 2), (2, 1), (3, 2), (2, 3), (1, 1), (3, 3), (1, 3),
    (3, 1), (0, 2), (2, 0), (0, 1), (1, 0), (0, 3), (3, 0), (0, 0),
)


def iota(shape, dim):
    return lax.broadcasted_iota(jnp.int32, shape, dim)


def base_table(freq_ref, f_of_row, r_of_row):
    shape = (16, NFFT)
    t = iota(shape, 1)
    bins = jnp.where(f_of_row == 0, freq_ref[0], freq_ref[1])
    phase = (bins * t + 64 * r_of_row) & (NFFT - 1)
    wave = jnp.cos(2.0 * math.pi * phase.astype(jnp.float32) / NFFT)
    hann = 0.5 - 0.5 * jnp.cos(2.0 * math.pi * t.astype(jnp.float32) / NFFT)
    return hann * (1.0 / math.sqrt(0.375 * NFFT)) * wave


def banded_table(freq_ref):
    row = iota((16, NFFT), 0)
    main = base_table(freq_ref, row // 8, (row // 4) % 2)
    halo = base_table(freq_ref, (row // 2) % 2, row % 2)
    j = iota((16, HOP), 0) % 4
    zero = jnp.zeros((16, HOP), jnp.float32)
    top = [
        jnp.where(j == q, main[:, :HOP], jnp.where(j == q - 1, main[:, HOP:], zero)) for q in range(OWN)
    ]
    bottom = [halo[:, HOP:], zero, zero, zero]
    return jnp.concatenate(
        [jnp.concatenate(top, axis=1), jnp.concatenate(bottom, axis=1)], axis=0
    ).astype(jnp.bfloat16)


def spread_matrices():
    out = iota((ROWS, 256), 0)
    src = iota((ROWS, 256), 1)
    f, r, s, j = out // 128, (out // 64) % 2, (out // 4) % 16, out % 4
    main = src == s * 16 + f * 8 + r * 4 + j
    tails = []
    for g in range(GROUPS):
        tails.append((j == 3) & (src == ((s + 1) % 16) * 16 + g * 4 + f * 2 + r))
    one = lambda m: jnp.where(m, 1.0, 0.0).astype(jnp.bfloat16)
    return one(main), [one(m) for m in tails]


def dot(a, b, contract=((1,), (0,))):
    return lax.dot_general(a, b, (contract, ((), ())), preferred_element_type=jnp.float32)


def gather_kernel(
    snap_ref, freq_ref, high_ref, low_ref, gram_ref,
    freq_buf, freq_sem, x_buf, send_buf, recv_buf, gpart, grecv, srecv,
    x_sem, send_sem, recv_sem, g_send, g_recv, s_send, s_recv, a_send, a_recv,
):
    sp = lax.axis_index("space")
    me = lax.axis_index("tm")
    z, y = me // 4, me % 4
    peers = [((z + dz) % 4) * 4 + (y + dy) % 4 for dz, dy in STEPS]
    mates = [(sp + k) % SPACE for k in range(1, SPACE)]

    barrier = pltpu.get_barrier_semaphore()
    for dest in peers[:-1]:
        pl.semaphore_signal(barrier, inc=1, device_id=(sp, dest), device_id_type=MESH)
    for mate in mates:
        pl.semaphore_signal(barrier, inc=1, device_id=(mate, me), device_id_type=MESH)

    bins = pltpu.make_async_copy(freq_ref, freq_buf, freq_sem)
    bins.start()
    loads = []
    for k, dest in enumerate(peers):
        cols = pl.ds(pl.multiple_of(dest * WIDTH, WIDTH), WIDTH)
        loads.append(pltpu.make_async_copy(snap_ref.at[:, cols], x_buf.at[k], x_sem.at[k]))
        loads[-1].start()

    bins.wait()
    table = banded_table(freq_buf)
    group = iota((16, PACK), 0) // 4
    sends = []
    for k, dest in enumerate(peers):
        loads[k].wait()
        rows = dot(table, x_buf[k])
        tail = rows[16:, :PACK]
        for g in range(1, GROUPS):
            tail = jnp.where(group == g, rows[16:, g * PACK : (g + 1) * PACK], tail)
        block = jnp.concatenate([rows[:16], tail], axis=1).astype(jnp.bfloat16)
        if k == TM - 1:
            recv_buf[me] = block
            break
        send_buf[k] = block
        copy = pltpu.make_async_remote_copy(
            src_ref=send_buf.at[k],
            dst_ref=recv_buf.at[me],
            send_sem=send_sem.at[k],
            recv_sem=recv_sem.at[k],
            device_id=(sp, dest),
            device_id_type=MESH,
        )
        sends.append(copy)
        if k == ENTER_AT:
            pl.semaphore_wait(barrier, TM - 1 + SPACE - 1)
            for early in sends:
                early.start()
        elif k > ENTER_AT:
            copy.start()

    main, tails = spread_matrices()
    for copy in sends:
        copy.wait_recv()

    extra = recv_buf[:, :, WIDTH:].reshape(ROWS, PACK)
    for g in range(GROUPS):
        lanes = slice(g * PACK, (g + 1) * PACK)
        got = recv_buf[:, :, lanes].reshape(ROWS, PACK)
        values = dot(main, got) + dot(tails[g], extra)
        high = values.astype(jnp.bfloat16)
        high_ref[:, lanes] = high
        low_ref[:, lanes] = (values - high.astype(jnp.float32)).astype(jnp.bfloat16)
    for f in range(NF):
        high = high_ref[f * COLS : (f + 1) * COLS, :]
        low = low_ref[f * COLS : (f + 1) * COLS, :]
        cross = dot(high, low, ((1,), (1,)))
        part = (dot(high, high, ((1,), (1,))) + (cross + cross.T)) * (1.0 / (WIDTH * TM * SPACE))
        gpart[f * 8 : (f + 1) * 8] = part.reshape(8, 16, COLS)

    copies = []
    for k, dest in enumerate(peers[:-1]):
        copy = pltpu.make_async_remote_copy(
            src_ref=gpart.at[dest],
            dst_ref=grecv.at[me],
            send_sem=g_send.at[k],
            recv_sem=g_recv.at[k],
            device_id=(sp, dest),
            device_id_type=MESH,
        )
        copy.start()
        copies.append(copy)
    grecv[me] = gpart[me]
    for copy in copies:
        copy.wait_recv()
    sends += copies
    srecv[sp] = jnp.sum(grecv[...], axis=0)

    copies = []
    for k, mate in enumerate(mates):
        copy = pltpu.make_async_remote_copy(
            src_ref=srecv.at[sp],
            dst_ref=srecv.at[sp],
            send_sem=s_send.at[k],
            recv_sem=s_recv.at[k],
            device_id=(mate, me),
            device_id_type=MESH,
        )
        copy.start()
        copies.append(copy)
    for copy in copies:
        copy.wait_recv()
    sends += copies
    gram_ref[me] = jnp.sum(srecv[...], axis=0)

    copies = []
    for k, dest in enumerate(peers[:-1]):
        copy = pltpu.make_async_remote_copy(
            src_ref=gram_ref.at[me],
            dst_ref=gram_ref.at[me],
            send_sem=a_send.at[k],
            recv_sem=a_recv.at[k],
            device_id=(sp, dest),
            device_id_type=MESH,
        )
        copy.start()
        copies.append(copy)
    for copy in copies:
        copy.wait_recv()
    sends += copies
    for copy in sends:
        copy.wait_send()


def split3(x):
    high = x.astype(jnp.bfloat16).astype(jnp.float32)
    rest = x - high
    mid = rest.astype(jnp.bfloat16).astype(jnp.float32)
    return high, mid, rest - mid


def lane(x, at):
    return jnp.broadcast_to(x[:, at : at + 1], x.shape)


def pair_rows(work_ref, at):
    one, two = (jnp.broadcast_to(work_ref[f, at : at + 1, :], (8, COLS)) for f in range(NF))
    return jnp.where(iota((8, COLS), 0) < 4, one, two)


def stack_rows(rows, f):
    sub = iota((8, COLS), 0) - 4 * f
    halves = []
    for part in (rows[:4], rows[4:]):
        half = part[0]
        for i in range(1, 4):
            half = jnp.where(sub == i, part[i], half)
        halves.append(half[4 * f : 4 * f + 4])
    return jnp.concatenate(halves, axis=0)


def factor_inverse(work_ref, inv_ref):
    at = iota((8, COLS), 1)
    for base in range(0, COLS, PANEL):
        rest = base + PANEL
        rows = [pair_rows(work_ref, base + i) for i in range(PANEL)]
        e = [[lane(rows[i], base + k) for k in range(i + 1)] for i in range(PANEL)]
        inside = (at >= base) & (at < rest)
        rows = [
            jnp.where(inside, jnp.where(at == base + i, 1.0, 0.0), rows[i]) for i in range(PANEL)
        ]
        scaled = [[None] * PANEL for _ in range(PANEL)]
        done = []
        for k in range(PANEL):
            for i in range(k, PANEL):
                for q in range(k):
                    e[i][k] = e[i][k] - scaled[k][q] * e[i][q]
            for q in range(k):
                rows[k] = rows[k] - scaled[k][q] * rows[q]
            inv = lax.rsqrt(e[k][k])
            inv2 = inv * inv
            done.append(rows[k] * inv)
            for i in range(k + 1, PANEL):
                scaled[i][k] = e[i][k] * inv2
        for f in range(NF):
            blocks = [stack_rows(done[q : q + 8], f) for q in range(0, PANEL, 8)]
            whole = jnp.concatenate(blocks, axis=0)
            lanes = iota((PANEL, COLS), 1)
            inv_ref[f, base:rest, :] = jnp.where(lanes < rest, whole, 0.0)
            if rest == COLS:
                continue
            h, m, l = split3(whole)
            left = jnp.concatenate([h, h, m, m, h, l], axis=0).astype(jnp.bfloat16)
            right = jnp.concatenate([h, m, h, m, l, h], axis=0).astype(jnp.bfloat16)
            update = dot(left, right, ((0,), (0,)))
            lower = work_ref[f, rest:, :]
            lanes = iota(lower.shape, 1)
            kept = jnp.where((lanes >= base) & (lanes < rest), 0.0, lower)
            work_ref[f, rest:, :] = kept - update[rest:, :]


def whiten_kernel(gram_in, high_ref, low_ref, gram_ref, out_ref, work_ref, inv_ref, out_buf, sem):
    gram_copy = pltpu.make_async_copy(gram_in, gram_ref, sem.at[NF])
    gram_copy.start()
    eye = jnp.where(iota((COLS, COLS), 0) == iota((COLS, COLS), 1), 1.0, 0.0)
    for f in range(NF):
        work_ref[f] = gram_in[f] + ridge_term * eye
    factor_inverse(work_ref, inv_ref)
    copies = []
    for f in range(NF):
        w = inv_ref[f]
        w_high = w.astype(jnp.bfloat16)
        w_low = (w - w_high.astype(jnp.float32)).astype(jnp.bfloat16)
        high = high_ref[f * COLS : (f + 1) * COLS, :]
        low = low_ref[f * COLS : (f + 1) * COLS, :]
        out_buf[f] = dot(w_high, high) + (dot(w_low, high) + dot(w_high, low))
        copies.append(pltpu.make_async_copy(out_buf.at[f], out_ref.at[f], sem.at[f]))
        copies[-1].start()
    gram_copy.wait()
    for copy in copies:
        copy.wait()


def on_device(snapshots, freq_bins):
    dma = pltpu.SemaphoreType.DMA
    hbm = pl.BlockSpec(memory_space=pltpu.HBM)
    vmem = pl.BlockSpec(memory_space=VMEM)
    high, low, gram = pl.pallas_call(
        gather_kernel,
        out_shape=[
            jax.ShapeDtypeStruct((ROWS, WIDTH), jnp.bfloat16),
            jax.ShapeDtypeStruct((ROWS, WIDTH), jnp.bfloat16),
            jax.ShapeDtypeStruct((TM, 16, COLS), jnp.float32),
        ],
        in_specs=[hbm, hbm],
        out_specs=[vmem, vmem, vmem],
        scratch_shapes=[
            pltpu.SMEM((NF,), jnp.int32),
            dma(()),
            VMEM((TM, TM * 32, WIDTH), jnp.bfloat16),
            VMEM((TM, 16, WIDTH + PACK), jnp.bfloat16),
            VMEM((TM, 16, WIDTH + PACK), jnp.bfloat16),
            VMEM((TM, 16, COLS), jnp.float32),
            VMEM((TM, 16, COLS), jnp.float32),
            VMEM((SPACE, 16, COLS), jnp.float32),
            dma((TM,)),
            dma((TM - 1,)),
            dma((TM - 1,)),
            dma((TM - 1,)),
            dma((TM - 1,)),
            dma((SPACE - 1,)),
            dma((SPACE - 1,)),
            dma((TM - 1,)),
            dma((TM - 1,)),
        ],
        compiler_params=pltpu.CompilerParams(
            collective_id=0, has_side_effects=True, vmem_limit_bytes=48 * 2**20
        ),
        name="gather",
    )(snapshots, pltpu.with_memory_space_constraint(freq_bins, pltpu.HBM))
    gram_matrix, whitened = pl.pallas_call(
        whiten_kernel,
        out_shape=[
            jax.ShapeDtypeStruct((NF, COLS, COLS), jnp.float32),
            jax.ShapeDtypeStruct((NF, COLS, WIDTH), jnp.float32),
        ],
        in_specs=[vmem, vmem, vmem],
        out_specs=[hbm, hbm],
        scratch_shapes=[
            VMEM((NF, COLS, COLS), jnp.float32),
            VMEM((NF, COLS, COLS), jnp.float32),
            VMEM((NF, COLS, WIDTH), jnp.float32),
            dma((NF + 1,)),
        ],
        compiler_params=pltpu.CompilerParams(vmem_limit_bytes=32 * 2**20),
        name="whiten",
    )(gram.reshape(NF, COLS, COLS), high, low)
    return gram_matrix, whitened


def solution(mesh):
    placed = (P("tm", "space"), P())
    return jax.shard_map(
        on_device,
        mesh=mesh,
        in_specs=placed,
        out_specs=(P(), P(None, None, ("space", "tm"))),
        check_vma=False,
    )
```

```python
import math

import jax
import jax.numpy as jnp
from jax import lax
from jax.experimental import pallas as pl
from jax.experimental.pallas import tpu as pltpu
from jax.sharding import PartitionSpec as P

NFFT = 256
HOP = 128
NF = 2
NB = 64
COLS = 2 * NB
ROWS = NF * COLS
TM = 16
SPACE = 8
OWN = NB // TM
WIDTH = 1024
GROUPS = 4
PACK = WIDTH // GROUPS
MESH = pl.DeviceIdType.MESH
VMEM = pltpu.VMEM
ridge_term = 0.01
ENTER_AT = 6
PANEL = 16
CUTS = (64, 96)

STEPS = (
    (2, 2), (1, 2), (2, 1), (3, 2), (2, 3), (1, 1), (3, 3), (1, 3),
    (3, 1), (0, 2), (2, 0), (0, 1), (1, 0), (0, 3), (3, 0), (0, 0),
)


def iota(shape, dim):
    return lax.broadcasted_iota(jnp.int32, shape, dim)


def base_table(freq_ref, f_of_row, r_of_row):
    shape = (16, NFFT)
    t = iota(shape, 1)
    bins = jnp.where(f_of_row == 0, freq_ref[0], freq_ref[1])
    phase = (bins * t + 64 * r_of_row) & (NFFT - 1)
    wave = jnp.cos(2.0 * math.pi * phase.astype(jnp.float32) / NFFT)
    hann = 0.5 - 0.5 * jnp.cos(2.0 * math.pi * t.astype(jnp.float32) / NFFT)
    return hann * (1.0 / math.sqrt(0.375 * NFFT)) * wave


def banded_table(freq_ref):
    row = iota((16, NFFT), 0)
    main = base_table(freq_ref, row // 8, (row // 4) % 2)
    halo = base_table(freq_ref, (row // 2) % 2, row % 2)
    j = iota((16, HOP), 0) % 4
    zero = jnp.zeros((16, HOP), jnp.float32)
    top = [
        jnp.where(j == q, main[:, :HOP], jnp.where(j == q - 1, main[:, HOP:], zero)) for q in range(OWN)
    ]
    bottom = [halo[:, HOP:], zero, zero, zero]
    return jnp.concatenate(
        [jnp.concatenate(top, axis=1), jnp.concatenate(bottom, axis=1)], axis=0
    ).astype(jnp.bfloat16)


def spread_matrices():
    out = iota((ROWS, 256), 0)
    src = iota((ROWS, 256), 1)
    f, r, s, j = out // 128, (out // 64) % 2, (out // 4) % 16, out % 4
    main = src == s * 16 + f * 8 + r * 4 + j
    tails = []
    for g in range(GROUPS):
        tails.append((j == 3) & (src == ((s + 1) % 16) * 16 + g * 4 + f * 2 + r))
    one = lambda m: jnp.where(m, 1.0, 0.0).astype(jnp.bfloat16)
    return one(main), [one(m) for m in tails]


def dot(a, b, contract=((1,), (0,))):
    return lax.dot_general(a, b, (contract, ((), ())), preferred_element_type=jnp.float32)


def gather_kernel(
    snap_ref, freq_ref, high_ref, low_ref, gram_ref,
    freq_buf, freq_sem, x_buf, send_buf, recv_buf, gpart, grecv, srecv,
    x_sem, send_sem, recv_sem, g_send, g_recv, s_send, s_recv, a_send, a_recv,
):
    sp = lax.axis_index("space")
    me = lax.axis_index("tm")
    z, y = me // 4, me % 4
    peers = [((z + dz) % 4) * 4 + (y + dy) % 4 for dz, dy in STEPS]
    mates = [(sp + k) % SPACE for k in range(1, SPACE)]

    barrier = pltpu.get_barrier_semaphore()
    for dest in peers[:-1]:
        pl.semaphore_signal(barrier, inc=1, device_id=(sp, dest), device_id_type=MESH)
    for mate in mates:
        pl.semaphore_signal(barrier, inc=1, device_id=(mate, me), device_id_type=MESH)

    bins = pltpu.make_async_copy(freq_ref, freq_buf, freq_sem)
    bins.start()
    loads = []
    for k, dest in enumerate(peers):
        cols = pl.ds(pl.multiple_of(dest * WIDTH, WIDTH), WIDTH)
        loads.append(pltpu.make_async_copy(snap_ref.at[:, cols], x_buf.at[k], x_sem.at[k]))
        loads[-1].start()

    bins.wait()
    table = banded_table(freq_buf)
    group = iota((16, PACK), 0) // 4
    sends = []
    for k, dest in enumerate(peers):
        loads[k].wait()
        rows = dot(table, x_buf[k])
        tail = rows[16:, :PACK]
        for g in range(1, GROUPS):
            tail = jnp.where(group == g, rows[16:, g * PACK : (g + 1) * PACK], tail)
        block = jnp.concatenate([rows[:16], tail], axis=1).astype(jnp.bfloat16)
        if k == TM - 1:
            recv_buf[me] = block
            break
        send_buf[k] = block
        copy = pltpu.make_async_remote_copy(
            src_ref=send_buf.at[k],
            dst_ref=recv_buf.at[me],
            send_sem=send_sem.at[k],
            recv_sem=recv_sem.at[k],
            device_id=(sp, dest),
            device_id_type=MESH,
        )
        sends.append(copy)
        if k == ENTER_AT:
            pl.semaphore_wait(barrier, TM - 1 + SPACE - 1)
            for early in sends:
                early.start()
        elif k > ENTER_AT:
            copy.start()

    main, tails = spread_matrices()
    for copy in sends:
        copy.wait_recv()

    extra = recv_buf[:, :, WIDTH:].reshape(ROWS, PACK)
    for g in range(GROUPS):
        lanes = slice(g * PACK, (g + 1) * PACK)
        got = recv_buf[:, :, lanes].reshape(ROWS, PACK)
        values = dot(main, got) + dot(tails[g], extra)
        high = values.astype(jnp.bfloat16)
        high_ref[:, lanes] = high
        low_ref[:, lanes] = (values - high.astype(jnp.float32)).astype(jnp.bfloat16)
    high, low = high_ref[...], low_ref[...]
    square = dot(high, high, ((1,), (1,)))
    cross = dot(high, low, ((1,), (1,)))
    parts = []
    for f in range(NF):
        own = slice(f * COLS, (f + 1) * COLS)
        mixed = cross[own, own]
        parts.append((square[own, own] + (mixed + mixed.T)) * (1.0 / (WIDTH * TM * SPACE)))
    i, j = iota((COLS, COLS), 0), iota((COLS, COLS), 1)
    gpart[:, :8, :] = jnp.where(j <= i, parts[0], parts[1]).reshape(TM, 8, COLS)
    diagonal = jnp.sum(jnp.where(i == j, parts[1], 0.0), axis=0, keepdims=True)
    for k in range(TM):
        gpart[k, 8:, :] = diagonal

    copies = []
    for k, dest in enumerate(peers[:-1]):
        copy = pltpu.make_async_remote_copy(
            src_ref=gpart.at[dest],
            dst_ref=grecv.at[me],
            send_sem=g_send.at[k],
            recv_sem=g_recv.at[k],
            device_id=(sp, dest),
            device_id_type=MESH,
        )
        copy.start()
        copies.append(copy)
    grecv[me] = gpart[me]
    for copy in copies:
        copy.wait_recv()
    sends += copies
    srecv[sp] = jnp.sum(grecv[...], axis=0)

    copies = []
    for k, mate in enumerate(mates):
        copy = pltpu.make_async_remote_copy(
            src_ref=srecv.at[sp],
            dst_ref=srecv.at[sp],
            send_sem=s_send.at[k],
            recv_sem=s_recv.at[k],
            device_id=(mate, me),
            device_id_type=MESH,
        )
        copy.start()
        copies.append(copy)
    for copy in copies:
        copy.wait_recv()
    sends += copies
    gram_ref[me] = jnp.sum(srecv[...], axis=0)

    copies = []
    for k, dest in enumerate(peers[:-1]):
        copy = pltpu.make_async_remote_copy(
            src_ref=gram_ref.at[me],
            dst_ref=gram_ref.at[me],
            send_sem=a_send.at[k],
            recv_sem=a_recv.at[k],
            device_id=(sp, dest),
            device_id_type=MESH,
        )
        copy.start()
        copies.append(copy)
    for copy in copies:
        copy.wait_recv()
    sends += copies
    for copy in sends:
        copy.wait_send()


def split3(x):
    high = x.astype(jnp.bfloat16).astype(jnp.float32)
    rest = x - high
    mid = rest.astype(jnp.bfloat16).astype(jnp.float32)
    return high, mid, rest - mid


def lane(x, at):
    return jnp.broadcast_to(x[:, at : at + 1], x.shape)


def pair_rows(work_ref, at):
    one, two = (jnp.broadcast_to(work_ref[f, at : at + 1, :], (8, COLS)) for f in range(NF))
    return jnp.where(iota((8, COLS), 0) < 4, one, two)


def stack_rows(rows, f):
    sub = iota((8, COLS), 0) - 4 * f
    halves = []
    for part in (rows[:4], rows[4:]):
        half = part[0]
        for i in range(1, 4):
            half = jnp.where(sub == i, part[i], half)
        halves.append(half[4 * f : 4 * f + 4])
    return jnp.concatenate(halves, axis=0)


def factor_inverse(work_ref, inv_ref, ready=None):
    at = iota((8, COLS), 1)
    for base in range(0, COLS, PANEL):
        rest = base + PANEL
        rows = [pair_rows(work_ref, base + i) for i in range(PANEL)]
        e = [[lane(rows[i], base + k) for k in range(i + 1)] for i in range(PANEL)]
        inside = (at >= base) & (at < rest)
        rows = [
            jnp.where(inside, jnp.where(at == base + i, 1.0, 0.0), rows[i]) for i in range(PANEL)
        ]
        scaled = [[None] * PANEL for _ in range(PANEL)]
        done = []
        for k in range(PANEL):
            for i in range(k, PANEL):
                for q in range(k):
                    e[i][k] = e[i][k] - scaled[k][q] * e[i][q]
            for q in range(k):
                rows[k] = rows[k] - scaled[k][q] * rows[q]
            inv = lax.rsqrt(e[k][k])
            inv2 = inv * inv
            done.append(rows[k] * inv)
            for i in range(k + 1, PANEL):
                scaled[i][k] = e[i][k] * inv2
        for f in range(NF):
            blocks = [stack_rows(done[q : q + 8], f) for q in range(0, PANEL, 8)]
            whole = jnp.concatenate(blocks, axis=0)
            lanes = iota((PANEL, COLS), 1)
            inv_ref[f, base:rest, :] = jnp.where(lanes < rest, whole, 0.0)
            if rest == COLS:
                continue
            h, m, l = split3(whole)
            left = jnp.concatenate([h, h, m, m, h, l], axis=0).astype(jnp.bfloat16)
            right = jnp.concatenate([h, m, h, m, l, h], axis=0).astype(jnp.bfloat16)
            update = dot(left, right, ((0,), (0,)))
            lower = work_ref[f, rest:, :]
            lanes = iota(lower.shape, 1)
            kept = jnp.where((lanes >= base) & (lanes < rest), 0.0, lower)
            work_ref[f, rest:, :] = kept - update[rest:, :]
        if ready is not None:
            ready(rest)


def whiten_kernel(gram_in, high_ref, low_ref, gram_ref, out_ref, work_ref, inv_ref, gram_buf, out_buf, sem):
    i, j = iota((COLS, COLS), 0), iota((COLS, COLS), 1)
    packed = gram_in[:, :8, :].reshape(COLS, COLS)
    turned = packed.T
    diagonal = jnp.broadcast_to(gram_in[0, 8:, :], (COLS, COLS))
    gram_buf[0] = jnp.where(j <= i, packed, turned)
    gram_buf[1] = jnp.where(j > i, packed, jnp.where(i == j, diagonal, turned))
    gram_copy = pltpu.make_async_copy(gram_buf, gram_ref, sem.at[8])
    gram_copy.start()
    for f in range(NF):
        work_ref[f] = gram_buf[f] + jnp.where(i == j, ridge_term, 0.0)
    copies = []

    def apply(f, lo, hi):
        w = inv_ref[f, lo:hi, :]
        w_high = w.astype(jnp.bfloat16)
        w_low = (w - w_high.astype(jnp.float32)).astype(jnp.bfloat16)
        high = high_ref[f * COLS : f * COLS + hi, :]
        low = low_ref[f * COLS : f * COLS + hi, :]
        w_high, w_low = w_high[:, :hi], w_low[:, :hi]
        out_buf[f, lo:hi] = dot(w_high, high) + (dot(w_low, high) + dot(w_high, low))
        copy = pltpu.make_async_copy(
            out_buf.at[f, lo:hi], out_ref.at[f, lo:hi], sem.at[len(copies)]
        )
        copy.start()
        copies.append(copy)

    def ready(rest):
        for lo, hi in zip((0,) + CUTS, CUTS + (COLS,)):
            if rest == hi:
                for f in range(NF):
                    apply(f, lo, hi)

    factor_inverse(work_ref, inv_ref, ready)
    gram_copy.wait()
    for copy in copies:
        copy.wait()


def on_device(snapshots, freq_bins):
    dma = pltpu.SemaphoreType.DMA
    hbm = pl.BlockSpec(memory_space=pltpu.HBM)
    vmem = pl.BlockSpec(memory_space=VMEM)
    high, low, gram = pl.pallas_call(
        gather_kernel,
        out_shape=[
            jax.ShapeDtypeStruct((ROWS, WIDTH), jnp.bfloat16),
            jax.ShapeDtypeStruct((ROWS, WIDTH), jnp.bfloat16),
            jax.ShapeDtypeStruct((TM, 9, COLS), jnp.float32),
        ],
        in_specs=[hbm, hbm],
        out_specs=[vmem, vmem, vmem],
        scratch_shapes=[
            pltpu.SMEM((NF,), jnp.int32),
            dma(()),
            VMEM((TM, TM * 32, WIDTH), jnp.bfloat16),
            VMEM((TM, 16, WIDTH + PACK), jnp.bfloat16),
            VMEM((TM, 16, WIDTH + PACK), jnp.bfloat16),
            VMEM((TM, 9, COLS), jnp.float32),
            VMEM((TM, 9, COLS), jnp.float32),
            VMEM((SPACE, 9, COLS), jnp.float32),
            dma((TM,)),
            dma((TM - 1,)),
            dma((TM - 1,)),
            dma((TM - 1,)),
            dma((TM - 1,)),
            dma((SPACE - 1,)),
            dma((SPACE - 1,)),
            dma((TM - 1,)),
            dma((TM - 1,)),
        ],
        compiler_params=pltpu.CompilerParams(
            collective_id=0, has_side_effects=True, vmem_limit_bytes=48 * 2**20
        ),
        name="gather",
    )(snapshots, pltpu.with_memory_space_constraint(freq_bins, pltpu.HBM))
    gram_matrix, whitened = pl.pallas_call(
        whiten_kernel,
        out_shape=[
            jax.ShapeDtypeStruct((NF, COLS, COLS), jnp.float32),
            jax.ShapeDtypeStruct((NF, COLS, WIDTH), jnp.float32),
        ],
        in_specs=[vmem, vmem, vmem],
        out_specs=[hbm, hbm],
        scratch_shapes=[
            VMEM((NF, COLS, COLS), jnp.float32),
            VMEM((NF, COLS, COLS), jnp.float32),
            VMEM((NF, COLS, COLS), jnp.float32),
            VMEM((NF, COLS, WIDTH), jnp.float32),
            dma((9,)),
        ],
        compiler_params=pltpu.CompilerParams(vmem_limit_bytes=32 * 2**20),
        name="whiten",
    )(gram, high, low)
    return gram_matrix, whitened


def solution(mesh):
    placed = (P("tm", "space"), P())
    return jax.shard_map(
        on_device,
        mesh=mesh,
        in_specs=placed,
        out_specs=(P(), P(None, None, ("space", "tm"))),
        check_vma=False,
    )
```

```python
import math

import jax
import jax.numpy as jnp
from jax import lax
from jax.experimental import pallas as pl
from jax.experimental.pallas import tpu as pltpu
from jax.sharding import PartitionSpec as P

NFFT = 256
HOP = 128
NF = 2
NB = 64
COLS = 2 * NB
ROWS = NF * COLS
TM = 16
SPACE = 8
OWN = NB // TM
WIDTH = 1024
GROUPS = 4
PACK = WIDTH // GROUPS
MESH = pl.DeviceIdType.MESH
VMEM = pltpu.VMEM
ridge_term = 0.01
ENTER_AT = 5
PANEL = 16
CUTS = (64, 96, 112)

STEPS = (
    (2, 2), (1, 2), (2, 1), (3, 2), (2, 3), (1, 1), (3, 3), (1, 3),
    (3, 1), (0, 2), (2, 0), (0, 1), (1, 0), (0, 3), (3, 0), (0, 0),
)


def iota(shape, dim):
    return lax.broadcasted_iota(jnp.int32, shape, dim)


def base_table(freq_ref, f_of_row, r_of_row):
    shape = (16, NFFT)
    t = iota(shape, 1)
    bins = jnp.where(f_of_row == 0, freq_ref[0], freq_ref[1])
    phase = (bins * t + 64 * r_of_row) & (NFFT - 1)
    wave = jnp.cos(2.0 * math.pi * phase.astype(jnp.float32) / NFFT)
    hann = 0.5 - 0.5 * jnp.cos(2.0 * math.pi * t.astype(jnp.float32) / NFFT)
    return hann * (1.0 / math.sqrt(0.375 * NFFT)) * wave


def banded_table(freq_ref):
    row = iota((16, NFFT), 0)
    main = base_table(freq_ref, row // 8, (row // 4) % 2)
    halo = base_table(freq_ref, (row // 2) % 2, row % 2)
    j = iota((16, HOP), 0) % 4
    zero = jnp.zeros((16, HOP), jnp.float32)
    top = [
        jnp.where(j == q, main[:, :HOP], jnp.where(j == q - 1, main[:, HOP:], zero)) for q in range(OWN)
    ]
    bottom = [halo[:, HOP:], zero, zero, zero]
    return jnp.concatenate(
        [jnp.concatenate(top, axis=1), jnp.concatenate(bottom, axis=1)], axis=0
    ).astype(jnp.bfloat16)


def spread_matrices():
    out = iota((ROWS, 256), 0)
    src = iota((ROWS, 256), 1)
    f, r, s, j = out // 128, (out // 64) % 2, (out // 4) % 16, out % 4
    main = src == s * 16 + f * 8 + r * 4 + j
    tails = []
    for g in range(GROUPS):
        tails.append((j == 3) & (src == ((s + 1) % 16) * 16 + g * 4 + f * 2 + r))
    one = lambda m: jnp.where(m, 1.0, 0.0).astype(jnp.bfloat16)
    return one(main), [one(m) for m in tails]


def dot(a, b, contract=((1,), (0,))):
    return lax.dot_general(a, b, (contract, ((), ())), preferred_element_type=jnp.float32)


def gather_kernel(
    snap_ref, freq_ref, high_ref, low_ref, gram_ref,
    freq_buf, freq_sem, x_buf, send_buf, recv_buf, gpart, grecv, srecv,
    x_sem, send_sem, recv_sem, g_send, g_recv, s_send, s_recv, a_send, a_recv,
):
    sp = lax.axis_index("space")
    me = lax.axis_index("tm")
    z, y = me // 4, me % 4
    peers = [((z + dz) % 4) * 4 + (y + dy) % 4 for dz, dy in STEPS]
    mates = [(sp + k) % SPACE for k in range(1, SPACE)]

    barrier = pltpu.get_barrier_semaphore()
    for dest in peers[:-1]:
        pl.semaphore_signal(barrier, inc=1, device_id=(sp, dest), device_id_type=MESH)
    for mate in mates:
        pl.semaphore_signal(barrier, inc=1, device_id=(mate, me), device_id_type=MESH)

    bins = pltpu.make_async_copy(freq_ref, freq_buf, freq_sem)
    bins.start()
    loads = []
    for k, dest in enumerate(peers):
        cols = pl.ds(pl.multiple_of(dest * WIDTH, WIDTH), WIDTH)
        loads.append(pltpu.make_async_copy(snap_ref.at[:, cols], x_buf.at[k], x_sem.at[k]))
        loads[-1].start()

    bins.wait()
    table = banded_table(freq_buf)
    group = iota((16, PACK), 0) // 4
    sends = []
    for k, dest in enumerate(peers):
        loads[k].wait()
        rows = dot(table, x_buf[k])
        tail = rows[16:, :PACK]
        for g in range(1, GROUPS):
            tail = jnp.where(group == g, rows[16:, g * PACK : (g + 1) * PACK], tail)
        block = jnp.concatenate([rows[:16], tail], axis=1).astype(jnp.bfloat16)
        if k == TM - 1:
            recv_buf[me] = block
            break
        send_buf[k] = block
        copy = pltpu.make_async_remote_copy(
            src_ref=send_buf.at[k],
            dst_ref=recv_buf.at[me],
            send_sem=send_sem.at[k],
            recv_sem=recv_sem.at[k],
            device_id=(sp, dest),
            device_id_type=MESH,
        )
        sends.append(copy)
        if k == ENTER_AT:
            pl.semaphore_wait(barrier, TM - 1 + SPACE - 1)
            for early in sends:
                early.start()
        elif k > ENTER_AT:
            copy.start()

    main, tails = spread_matrices()
    for copy in sends:
        copy.wait_recv()

    extra = recv_buf[:, :, WIDTH:].reshape(ROWS, PACK)
    for g in range(GROUPS):
        lanes = slice(g * PACK, (g + 1) * PACK)
        got = recv_buf[:, :, lanes].reshape(ROWS, PACK)
        values = dot(main, got) + dot(tails[g], extra)
        high = values.astype(jnp.bfloat16)
        high_ref[:, lanes] = high
        low_ref[:, lanes] = (values - high.astype(jnp.float32)).astype(jnp.bfloat16)
    high, low = high_ref[...], low_ref[...]
    square = dot(high, high, ((1,), (1,)))
    cross = dot(high, low, ((1,), (1,)))
    parts = []
    for f in range(NF):
        own = slice(f * COLS, (f + 1) * COLS)
        mixed = cross[own, own]
        parts.append((square[own, own] + (mixed + mixed.T)) * (1.0 / (WIDTH * TM * SPACE)))
    i, j = iota((COLS, COLS), 0), iota((COLS, COLS), 1)
    gpart[:, :8, :] = jnp.where(j <= i, parts[0], parts[1]).reshape(TM, 8, COLS)
    diagonal = jnp.sum(jnp.where(i == j, parts[1], 0.0), axis=0, keepdims=True)
    for k in range(TM):
        gpart[k, 8:, :] = diagonal

    copies = []
    for k, dest in enumerate(peers[:-1]):
        copy = pltpu.make_async_remote_copy(
            src_ref=gpart.at[dest],
            dst_ref=grecv.at[me],
            send_sem=g_send.at[k],
            recv_sem=g_recv.at[k],
            device_id=(sp, dest),
            device_id_type=MESH,
        )
        copy.start()
        copies.append(copy)
    grecv[me] = gpart[me]
    for copy in copies:
        copy.wait_recv()
    sends += copies
    srecv[sp] = jnp.sum(grecv[...], axis=0)

    copies = []
    for k, mate in enumerate(mates):
        copy = pltpu.make_async_remote_copy(
            src_ref=srecv.at[sp],
            dst_ref=srecv.at[sp],
            send_sem=s_send.at[k],
            recv_sem=s_recv.at[k],
            device_id=(mate, me),
            device_id_type=MESH,
        )
        copy.start()
        copies.append(copy)
    for copy in copies:
        copy.wait_recv()
    sends += copies
    gram_ref[me] = jnp.sum(srecv[...], axis=0)

    copies = []
    for k, dest in enumerate(peers[:-1]):
        copy = pltpu.make_async_remote_copy(
            src_ref=gram_ref.at[me],
            dst_ref=gram_ref.at[me],
            send_sem=a_send.at[k],
            recv_sem=a_recv.at[k],
            device_id=(sp, dest),
            device_id_type=MESH,
        )
        copy.start()
        copies.append(copy)
    for copy in copies:
        copy.wait_recv()
    sends += copies
    for copy in sends:
        copy.wait_send()


def split3(x):
    high = x.astype(jnp.bfloat16).astype(jnp.float32)
    rest = x - high
    mid = rest.astype(jnp.bfloat16).astype(jnp.float32)
    return high, mid, rest - mid


def lane(x, at):
    return jnp.broadcast_to(x[:, at : at + 1], x.shape)


def pair_rows(work_ref, at):
    one, two = (jnp.broadcast_to(work_ref[f, at : at + 1, :], (8, COLS)) for f in range(NF))
    return jnp.where(iota((8, COLS), 0) < 4, one, two)


def stack_rows(rows, f):
    sub = iota((8, COLS), 0) - 4 * f
    halves = []
    for part in (rows[:4], rows[4:]):
        half = part[0]
        for i in range(1, 4):
            half = jnp.where(sub == i, part[i], half)
        halves.append(half[4 * f : 4 * f + 4])
    return jnp.concatenate(halves, axis=0)


def factor_inverse(work_ref, inv_ref, ready=None):
    at = iota((8, COLS), 1)
    for base in range(0, COLS, PANEL):
        rest = base + PANEL
        rows = [pair_rows(work_ref, base + i) for i in range(PANEL)]
        e = [[lane(rows[i], base + k) for k in range(i + 1)] for i in range(PANEL)]
        inside = (at >= base) & (at < rest)
        rows = [
            jnp.where(inside, jnp.where(at == base + i, 1.0, 0.0), rows[i]) for i in range(PANEL)
        ]
        scaled = [[None] * PANEL for _ in range(PANEL)]
        done = []
        for k in range(PANEL):
            for i in range(k, PANEL):
                for q in range(k):
                    e[i][k] = e[i][k] - scaled[k][q] * e[i][q]
            for q in range(k):
                rows[k] = rows[k] - scaled[k][q] * rows[q]
            inv = lax.rsqrt(e[k][k])
            inv2 = inv * inv
            done.append(rows[k] * inv)
            for i in range(k + 1, PANEL):
                scaled[i][k] = e[i][k] * inv2
        for f in range(NF):
            blocks = [stack_rows(done[q : q + 8], f) for q in range(0, PANEL, 8)]
            whole = jnp.concatenate(blocks, axis=0)
            lanes = iota((PANEL, COLS), 1)
            inv_ref[f, base:rest, :] = jnp.where(lanes < rest, whole, 0.0)
            if rest == COLS:
                continue
            h, m, l = split3(whole)
            left = jnp.concatenate([h, h, m, m, h, l], axis=0).astype(jnp.bfloat16)
            right = jnp.concatenate([h, m, h, m, l, h], axis=0).astype(jnp.bfloat16)
            update = dot(left, right, ((0,), (0,)))
            lower = work_ref[f, rest:, :]
            lanes = iota(lower.shape, 1)
            kept = jnp.where((lanes >= base) & (lanes < rest), 0.0, lower)
            work_ref[f, rest:, :] = kept - update[rest:, :]
        if ready is not None:
            ready(rest)


def whiten_kernel(gram_in, high_ref, low_ref, gram_ref, out_ref, work_ref, inv_ref, gram_buf, out_buf, sem):
    i, j = iota((COLS, COLS), 0), iota((COLS, COLS), 1)
    packed = gram_in[:, :8, :].reshape(COLS, COLS)
    turned = packed.T
    diagonal = jnp.broadcast_to(gram_in[0, 8:, :], (COLS, COLS))
    gram_buf[0] = jnp.where(j <= i, packed, turned)
    gram_buf[1] = jnp.where(j > i, packed, jnp.where(i == j, diagonal, turned))
    gram_copy = pltpu.make_async_copy(gram_buf, gram_ref, sem.at[8])
    gram_copy.start()
    for f in range(NF):
        work_ref[f] = gram_buf[f] + jnp.where(i == j, ridge_term, 0.0)
    copies = []

    def apply(f, lo, hi):
        w = inv_ref[f, lo:hi, :]
        w_high = w.astype(jnp.bfloat16)
        w_low = (w - w_high.astype(jnp.float32)).astype(jnp.bfloat16)
        high = high_ref[f * COLS : f * COLS + hi, :]
        low = low_ref[f * COLS : f * COLS + hi, :]
        w_high, w_low = w_high[:, :hi], w_low[:, :hi]
        out_buf[f, lo:hi] = dot(w_high, high) + (dot(w_low, high) + dot(w_high, low))
        copy = pltpu.make_async_copy(
            out_buf.at[f, lo:hi], out_ref.at[f, lo:hi], sem.at[len(copies)]
        )
        copy.start()
        copies.append(copy)

    def ready(rest):
        for lo, hi in zip((0,) + CUTS, CUTS + (COLS,)):
            if rest == hi:
                for f in range(NF):
                    apply(f, lo, hi)

    factor_inverse(work_ref, inv_ref, ready)
    gram_copy.wait()
    for copy in copies:
        copy.wait()


def on_device(snapshots, freq_bins):
    dma = pltpu.SemaphoreType.DMA
    hbm = pl.BlockSpec(memory_space=pltpu.HBM)
    vmem = pl.BlockSpec(memory_space=VMEM)
    high, low, gram = pl.pallas_call(
        gather_kernel,
        out_shape=[
            jax.ShapeDtypeStruct((ROWS, WIDTH), jnp.bfloat16),
            jax.ShapeDtypeStruct((ROWS, WIDTH), jnp.bfloat16),
            jax.ShapeDtypeStruct((TM, 9, COLS), jnp.float32),
        ],
        in_specs=[hbm, hbm],
        out_specs=[vmem, vmem, vmem],
        scratch_shapes=[
            pltpu.SMEM((NF,), jnp.int32),
            dma(()),
            VMEM((TM, TM * 32, WIDTH), jnp.bfloat16),
            VMEM((TM, 16, WIDTH + PACK), jnp.bfloat16),
            VMEM((TM, 16, WIDTH + PACK), jnp.bfloat16),
            VMEM((TM, 9, COLS), jnp.float32),
            VMEM((TM, 9, COLS), jnp.float32),
            VMEM((SPACE, 9, COLS), jnp.float32),
            dma((TM,)),
            dma((TM - 1,)),
            dma((TM - 1,)),
            dma((TM - 1,)),
            dma((TM - 1,)),
            dma((SPACE - 1,)),
            dma((SPACE - 1,)),
            dma((TM - 1,)),
            dma((TM - 1,)),
        ],
        compiler_params=pltpu.CompilerParams(
            collective_id=0, has_side_effects=True, vmem_limit_bytes=48 * 2**20
        ),
        name="gather",
    )(snapshots, pltpu.with_memory_space_constraint(freq_bins, pltpu.HBM))
    gram_matrix, whitened = pl.pallas_call(
        whiten_kernel,
        out_shape=[
            jax.ShapeDtypeStruct((NF, COLS, COLS), jnp.float32),
            jax.ShapeDtypeStruct((NF, COLS, WIDTH), jnp.float32),
        ],
        in_specs=[vmem, vmem, vmem],
        out_specs=[hbm, hbm],
        scratch_shapes=[
            VMEM((NF, COLS, COLS), jnp.float32),
            VMEM((NF, COLS, COLS), jnp.float32),
            VMEM((NF, COLS, COLS), jnp.float32),
            VMEM((NF, COLS, WIDTH), jnp.float32),
            dma((9,)),
        ],
        compiler_params=pltpu.CompilerParams(vmem_limit_bytes=32 * 2**20),
        name="whiten",
    )(gram, high, low)
    return gram_matrix, whitened


def solution(mesh):
    placed = (P("tm", "space"), P())
    return jax.shard_map(
        on_device,
        mesh=mesh,
        in_specs=placed,
        out_specs=(P(), P(None, None, ("space", "tm"))),
        check_vma=False,
    )
```

```python
import math

import jax
import jax.numpy as jnp
from jax import lax
from jax.experimental import pallas as pl
from jax.experimental.pallas import tpu as pltpu
from jax.sharding import PartitionSpec as P

NFFT = 256
HOP = 128
NF = 2
NB = 64
COLS = 2 * NB
ROWS = NF * COLS
TM = 16
SPACE = 8
OWN = NB // TM
WIDTH = 1024
GROUPS = 4
PACK = WIDTH // GROUPS
MESH = pl.DeviceIdType.MESH
VMEM = pltpu.VMEM
ridge_term = 0.01
ENTER_AT = 5
PANEL = 16
CUTS = (64, 96, 112)

STEPS = (
    (2, 2), (1, 2), (2, 1), (3, 2), (2, 3), (1, 1), (3, 3), (1, 3),
    (3, 1), (0, 2), (2, 0), (0, 1), (1, 0), (0, 3), (3, 0), (0, 0),
)


def iota(shape, dim):
    return lax.broadcasted_iota(jnp.int32, shape, dim)


def base_table(freq_ref, f_of_row, r_of_row):
    shape = (16, NFFT)
    t = iota(shape, 1)
    bins = jnp.where(f_of_row == 0, freq_ref[0], freq_ref[1])
    phase = (bins * t + 64 * r_of_row) & (NFFT - 1)
    wave = jnp.cos(2.0 * math.pi * phase.astype(jnp.float32) / NFFT)
    hann = 0.5 - 0.5 * jnp.cos(2.0 * math.pi * t.astype(jnp.float32) / NFFT)
    return hann * (1.0 / math.sqrt(0.375 * NFFT)) * wave


def banded_table(freq_ref):
    row = iota((16, NFFT), 0)
    main = base_table(freq_ref, row // 8, (row // 4) % 2)
    halo = base_table(freq_ref, (row // 2) % 2, row % 2)
    j = iota((16, HOP), 0) % 4
    zero = jnp.zeros((16, HOP), jnp.float32)
    top = [
        jnp.where(j == q, main[:, :HOP], jnp.where(j == q - 1, main[:, HOP:], zero)) for q in range(OWN)
    ]
    bottom = [halo[:, HOP:], zero, zero, zero]
    return jnp.concatenate(
        [jnp.concatenate(top, axis=1), jnp.concatenate(bottom, axis=1)], axis=0
    ).astype(jnp.bfloat16)


def spread_matrices():
    out = iota((ROWS, 256), 0)
    src = iota((ROWS, 256), 1)
    f, r, s, j = out // 128, (out // 64) % 2, (out // 4) % 16, out % 4
    main = src == s * 16 + f * 8 + r * 4 + j
    tails = []
    for g in range(GROUPS):
        tails.append((j == 3) & (src == ((s + 1) % 16) * 16 + g * 4 + f * 2 + r))
    one = lambda m: jnp.where(m, 1.0, 0.0).astype(jnp.bfloat16)
    return one(main), [one(m) for m in tails]


def dot(a, b, contract=((1,), (0,))):
    return lax.dot_general(a, b, (contract, ((), ())), preferred_element_type=jnp.float32)


def gather_kernel(
    snap_ref, freq_ref, high_ref, low_ref, gram_ref,
    freq_buf, freq_sem, x_buf, send_buf, recv_buf, gpart, grecv, srecv,
    x_sem, send_sem, recv_sem, g_send, g_recv, s_send, s_recv, a_send, a_recv,
):
    sp = lax.axis_index("space")
    me = lax.axis_index("tm")
    z, y = me // 4, me % 4
    peers = [((z + dz) % 4) * 4 + (y + dy) % 4 for dz, dy in STEPS]
    mates = [(sp + k) % SPACE for k in range(1, SPACE)]

    barrier = pltpu.get_barrier_semaphore()
    for dest in peers[:-1]:
        pl.semaphore_signal(barrier, inc=1, device_id=(sp, dest), device_id_type=MESH)
    for mate in mates:
        pl.semaphore_signal(barrier, inc=1, device_id=(mate, me), device_id_type=MESH)

    bins = pltpu.make_async_copy(freq_ref, freq_buf, freq_sem)
    bins.start()
    loads = []
    for k, dest in enumerate(peers):
        cols = pl.ds(pl.multiple_of(dest * WIDTH, WIDTH), WIDTH)
        loads.append(pltpu.make_async_copy(snap_ref.at[:, cols], x_buf.at[k], x_sem.at[k]))
        loads[-1].start()

    bins.wait()
    table = banded_table(freq_buf)
    group = iota((16, PACK), 0) // 4
    sends = []
    for k, dest in enumerate(peers):
        loads[k].wait()
        rows = dot(table, x_buf[k])
        tail = rows[16:, :PACK]
        for g in range(1, GROUPS):
            tail = jnp.where(group == g, rows[16:, g * PACK : (g + 1) * PACK], tail)
        block = jnp.concatenate([rows[:16], tail], axis=1).astype(jnp.bfloat16)
        if k == TM - 1:
            recv_buf[me] = block
            break
        send_buf[k] = block
        copy = pltpu.make_async_remote_copy(
            src_ref=send_buf.at[k],
            dst_ref=recv_buf.at[me],
            send_sem=send_sem.at[k],
            recv_sem=recv_sem.at[k],
            device_id=(sp, dest),
            device_id_type=MESH,
        )
        sends.append(copy)
        if k == ENTER_AT:
            pl.semaphore_wait(barrier, TM - 1 + SPACE - 1)
            for early in sends:
                early.start()
        elif k > ENTER_AT:
            copy.start()

    main, tails = spread_matrices()
    for copy in sends:
        copy.wait_recv()

    extra = recv_buf[:, :, WIDTH:].reshape(ROWS, PACK)
    for g in range(GROUPS):
        lanes = slice(g * PACK, (g + 1) * PACK)
        got = recv_buf[:, :, lanes].reshape(ROWS, PACK)
        values = dot(main, got) + dot(tails[g], extra)
        high = values.astype(jnp.bfloat16)
        high_ref[:, lanes] = high
        low_ref[:, lanes] = (values - high.astype(jnp.float32)).astype(jnp.bfloat16)
    high, low = high_ref[...], low_ref[...]
    square = dot(high, high, ((1,), (1,)))
    cross = dot(high, low, ((1,), (1,)))
    parts = []
    for f in range(NF):
        own = slice(f * COLS, (f + 1) * COLS)
        mixed = cross[own, own]
        parts.append((square[own, own] + (mixed + mixed.T)) * (1.0 / (WIDTH * TM * SPACE)))
    i, j = iota((COLS, COLS), 0), iota((COLS, COLS), 1)
    gpart[:, :8, :] = jnp.where(j <= i, parts[0], parts[1]).reshape(TM, 8, COLS)
    diagonal = jnp.sum(jnp.where(i == j, parts[1], 0.0), axis=0, keepdims=True)
    for k in range(TM):
        gpart[k, 8:, :] = diagonal

    copies = []
    for k, dest in enumerate(peers[:-1]):
        copy = pltpu.make_async_remote_copy(
            src_ref=gpart.at[dest],
            dst_ref=grecv.at[me],
            send_sem=g_send.at[k],
            recv_sem=g_recv.at[k],
            device_id=(sp, dest),
            device_id_type=MESH,
        )
        copy.start()
        copies.append(copy)
    grecv[me] = gpart[me]
    for copy in copies:
        copy.wait_recv()
    sends += copies
    srecv[sp] = jnp.sum(grecv[...], axis=0)

    copies = []
    for k, mate in enumerate(mates):
        copy = pltpu.make_async_remote_copy(
            src_ref=srecv.at[sp],
            dst_ref=srecv.at[sp],
            send_sem=s_send.at[k],
            recv_sem=s_recv.at[k],
            device_id=(mate, me),
            device_id_type=MESH,
        )
        copy.start()
        copies.append(copy)
    for copy in copies:
        copy.wait_recv()
    sends += copies
    gram_ref[me] = jnp.sum(srecv[...], axis=0)

    copies = []
    for k, dest in enumerate(peers[:-1]):
        copy = pltpu.make_async_remote_copy(
            src_ref=gram_ref.at[me],
            dst_ref=gram_ref.at[me],
            send_sem=a_send.at[k],
            recv_sem=a_recv.at[k],
            device_id=(sp, dest),
            device_id_type=MESH,
        )
        copy.start()
        copies.append(copy)
    for copy in sends:
        copy.wait_send()
    for copy in copies:
        copy.wait_recv()
    for copy in copies:
        copy.wait_send()


def split3(x):
    high = x.astype(jnp.bfloat16).astype(jnp.float32)
    rest = x - high
    mid = rest.astype(jnp.bfloat16).astype(jnp.float32)
    return high, mid, rest - mid


def lane(x, at):
    return jnp.broadcast_to(x[:, at : at + 1], x.shape)


def pair_rows(work_ref, at):
    one, two = (jnp.broadcast_to(work_ref[f, at : at + 1, :], (8, COLS)) for f in range(NF))
    return jnp.where(iota((8, COLS), 0) < 4, one, two)


def stack_rows(rows, f):
    sub = iota((8, COLS), 0) - 4 * f
    halves = []
    for part in (rows[:4], rows[4:]):
        half = part[0]
        for i in range(1, 4):
            half = jnp.where(sub == i, part[i], half)
        halves.append(half[4 * f : 4 * f + 4])
    return jnp.concatenate(halves, axis=0)


def factor_inverse(work_ref, inv_ref, ready=None):
    at = iota((8, COLS), 1)
    for base in range(0, COLS, PANEL):
        rest = base + PANEL
        rows = [pair_rows(work_ref, base + i) for i in range(PANEL)]
        e = [[lane(rows[i], base + k) for k in range(i + 1)] for i in range(PANEL)]
        inside = (at >= base) & (at < rest)
        rows = [
            jnp.where(inside, jnp.where(at == base + i, 1.0, 0.0), rows[i]) for i in range(PANEL)
        ]
        scaled = [[None] * PANEL for _ in range(PANEL)]
        done = []
        for k in range(PANEL):
            for i in range(k, PANEL):
                for q in range(k):
                    e[i][k] = e[i][k] - scaled[k][q] * e[i][q]
            for q in range(k):
                rows[k] = rows[k] - scaled[k][q] * rows[q]
            inv = lax.rsqrt(e[k][k])
            inv2 = inv * inv
            done.append(rows[k] * inv)
            for i in range(k + 1, PANEL):
                scaled[i][k] = e[i][k] * inv2
        for f in range(NF):
            blocks = [stack_rows(done[q : q + 8], f) for q in range(0, PANEL, 8)]
            whole = jnp.concatenate(blocks, axis=0)
            lanes = iota((PANEL, COLS), 1)
            inv_ref[f, base:rest, :] = jnp.where(lanes < rest, whole, 0.0)
            if rest == COLS:
                continue
            h, m, l = split3(whole)
            left = jnp.concatenate([h, h, m, m, h, l], axis=0).astype(jnp.bfloat16)
            right = jnp.concatenate([h, m, h, m, l, h], axis=0).astype(jnp.bfloat16)
            update = dot(left, right, ((0,), (0,)))
            lower = work_ref[f, rest:, :]
            lanes = iota(lower.shape, 1)
            kept = jnp.where((lanes >= base) & (lanes < rest), 0.0, lower)
            work_ref[f, rest:, :] = kept - update[rest:, :]
        if ready is not None:
            ready(rest)


def whiten_kernel(gram_in, high_ref, low_ref, gram_ref, out_ref, work_ref, inv_ref, gram_buf, out_buf, sem):
    i, j = iota((COLS, COLS), 0), iota((COLS, COLS), 1)
    packed = gram_in[:, :8, :].reshape(COLS, COLS)
    turned = packed.T
    diagonal = jnp.broadcast_to(gram_in[0, 8:, :], (COLS, COLS))
    gram_buf[0] = jnp.where(j <= i, packed, turned)
    gram_buf[1] = jnp.where(j > i, packed, jnp.where(i == j, diagonal, turned))
    gram_copy = pltpu.make_async_copy(gram_buf, gram_ref, sem.at[8])
    gram_copy.start()
    for f in range(NF):
        work_ref[f] = gram_buf[f] + jnp.where(i == j, ridge_term, 0.0)
    copies = []

    def apply(f, lo, hi):
        w = inv_ref[f, lo:hi, :]
        w_high = w.astype(jnp.bfloat16)
        w_low = (w - w_high.astype(jnp.float32)).astype(jnp.bfloat16)
        high = high_ref[f * COLS : f * COLS + hi, :]
        low = low_ref[f * COLS : f * COLS + hi, :]
        w_high, w_low = w_high[:, :hi], w_low[:, :hi]
        out_buf[f, lo:hi] = dot(w_high, high) + (dot(w_low, high) + dot(w_high, low))
        copy = pltpu.make_async_copy(
            out_buf.at[f, lo:hi], out_ref.at[f, lo:hi], sem.at[len(copies)]
        )
        copy.start()
        copies.append(copy)

    def ready(rest):
        for lo, hi in zip((0,) + CUTS, CUTS + (COLS,)):
            if rest == hi:
                for f in range(NF):
                    apply(f, lo, hi)

    factor_inverse(work_ref, inv_ref, ready)
    gram_copy.wait()
    for copy in copies:
        copy.wait()


def on_device(snapshots, freq_bins):
    dma = pltpu.SemaphoreType.DMA
    hbm = pl.BlockSpec(memory_space=pltpu.HBM)
    vmem = pl.BlockSpec(memory_space=VMEM)
    high, low, gram = pl.pallas_call(
        gather_kernel,
        out_shape=[
            jax.ShapeDtypeStruct((ROWS, WIDTH), jnp.bfloat16),
            jax.ShapeDtypeStruct((ROWS, WIDTH), jnp.bfloat16),
            jax.ShapeDtypeStruct((TM, 9, COLS), jnp.float32),
        ],
        in_specs=[hbm, hbm],
        out_specs=[vmem, vmem, vmem],
        scratch_shapes=[
            pltpu.SMEM((NF,), jnp.int32),
            dma(()),
            VMEM((TM, TM * 32, WIDTH), jnp.bfloat16),
            VMEM((TM, 16, WIDTH + PACK), jnp.bfloat16),
            VMEM((TM, 16, WIDTH + PACK), jnp.bfloat16),
            VMEM((TM, 9, COLS), jnp.float32),
            VMEM((TM, 9, COLS), jnp.float32),
            VMEM((SPACE, 9, COLS), jnp.float32),
            dma((TM,)),
            dma((TM - 1,)),
            dma((TM - 1,)),
            dma((TM - 1,)),
            dma((TM - 1,)),
            dma((SPACE - 1,)),
            dma((SPACE - 1,)),
            dma((TM - 1,)),
            dma((TM - 1,)),
        ],
        compiler_params=pltpu.CompilerParams(
            collective_id=0, has_side_effects=True, vmem_limit_bytes=48 * 2**20
        ),
        name="gather",
    )(snapshots, pltpu.with_memory_space_constraint(freq_bins, pltpu.HBM))
    gram_matrix, whitened = pl.pallas_call(
        whiten_kernel,
        out_shape=[
            jax.ShapeDtypeStruct((NF, COLS, COLS), jnp.float32),
            jax.ShapeDtypeStruct((NF, COLS, WIDTH), jnp.float32),
        ],
        in_specs=[vmem, vmem, vmem],
        out_specs=[hbm, hbm],
        scratch_shapes=[
            VMEM((NF, COLS, COLS), jnp.float32),
            VMEM((NF, COLS, COLS), jnp.float32),
            VMEM((NF, COLS, COLS), jnp.float32),
            VMEM((NF, COLS, WIDTH), jnp.float32),
            dma((9,)),
        ],
        compiler_params=pltpu.CompilerParams(vmem_limit_bytes=32 * 2**20),
        name="whiten",
    )(gram, high, low)
    return gram_matrix, whitened


def solution(mesh):
    placed = (P("tm", "space"), P())
    return jax.shard_map(
        on_device,
        mesh=mesh,
        in_specs=placed,
        out_specs=(P(), P(None, None, ("space", "tm"))),
        check_vma=False,
    )
```
